32 devices in a mesh: group: 2 (over y), tensor: 4 (over z), job: 4 (over x, core).
Axes of the slice: x: 2, y: 2, z: 4, core: 2. Of those that a mesh axis runs over, the one named last changes fastest.
Arguments:
- hidden: bfloat16 [1024, 28672], P(('group', 'job'), 'tensor'), parts along dimension 0, may hold values from -6 to 6
- frozen_down_weight: bfloat16 [28672, 8192], P('tensor', 'job'), may hold values from -0.03125 to 0.03125
- adapter_down_matrices: bfloat16 [16, 28672, 64], P(('group', 'job'), 'tensor'), parts along dimension 0, may hold values from -0.03125 to 0.03125
- adapter_up_matrices: bfloat16 [16, 64, 8192], P(('group', 'tensor'), None, 'job'), parts along dimension 0, may hold values from -0.75 to 0.75
- row_block_job_ids: int32 [8], P('group'), parts along dimension 0, may hold values from 0 to 7
- home: int32 [16], P('group'), parts along dimension 0, may hold values from 0 to 7, each once
- cotangent: bfloat16 [1024, 8192], P(('group', 'tensor'), 'job'), parts along dimension 0, may hold values from -6 to 6
Outputs:
- mixed: bfloat16 [1024, 8192], P(('group', 'tensor'), 'job'), parts along dimension 0
- hidden_gradient: bfloat16 [1024, 28672], P(('group', 'job'), 'tensor'), parts along dimension 0
- grad_down: bfloat16 [16, 28672, 64], P(('group', 'job'), 'tensor'), parts along dimension 0
- up_matrix_gradient: bfloat16 [16, 64, 8192], P(('group', 'tensor'), None, 'job'), parts along dimension 0
The draws below stay inside these ranges and needn't reach their ends.
There are 2 independent parts, one for each index of `group`. The reference program is written for one: setup_inputs(seed, part) draws one part's arguments, and reference() takes and returns one part's arrays. A program takes and returns all parts, laid end to end along the dimension named above; an argument that names none is the same for every part. Nothing has to cross between parts.
Inputs may be any that keep to these rules, and one draw needn't show every extreme that they name: `home`: each job names a different storage row; row s of adapter_down_matrices and grad_down lies on the job index that holds row s in their placement, row s of adapter_up_matrices and up_matrix_gradient on the tensor index that holds it in theirs.
All inputs are finite; a program needn't handle non-finite values.
Results may differ from the reference program's by a relative error of at most 0.014.
Values may be sent and summed in bfloat16 or wider, within the bound.
A program may use at most 192 MiB of HBM per device.

```python
import math
import jax
import jax.numpy as jnp
import numpy as np
from jax import lax

MODEL_WIDTH = 8192
HIDDEN_UNITS = 28672
ADAPTER_RANK = 64
BLOCK = 128
ADAPTER_JOBS = 8
BLOCKS = 4
TOTAL_ROWS = 512
N_TENSOR = 4
N_JOB = 4


def place_ends(values, key, least, high):
    longest = values.shape.index(max(values.shape))
    spots = []
    for shift in (0, 1):
        where = [jax.random.randint(jax.random.fold_in(key, axis), (), 0, length) for axis, length in enumerate(values.shape)]
        where[longest] = (where[longest] + shift) % values.shape[longest]
        spots.append(tuple(where))
    return values.at[spots[0]].set(least).at[spots[1]].set(high)


def steps_of(key, shape, cuts, smallest, top_value):
    def one(dim, shards_of):
        heights = jax.random.uniform(jax.random.fold_in(jax.random.fold_in(key, 6), dim), (shards_of,), jnp.float32, smallest / len(cuts), top_value / len(cuts))
        return jnp.repeat(jnp.exp(heights), shape[dim] // shards_of).reshape((-1,) + (1,) * (len(shape) - dim - 1))

    level = one(*cuts[0])
    for cut in cuts[1:]:
        level = level * one(*cut)
    return level


def rank_bounds(count, slope):
    loads = [(1 << 20) // math.isqrt(rank ** slope) + 1 for rank in range(1, count + 1)]
    width = 1 + sum(loads) // (1 << 30)
    return np.cumsum(np.array([max(1, weight // width) for weight in loads]))


def ranked_ids(stream_key, shape, count, skew):
    listing = rank_bounds(count, skew)
    pick = jax.random.randint(jax.random.fold_in(stream_key, 1), shape, 0, int(listing[count - 1]))
    rank = jnp.searchsorted(jnp.asarray(listing, jnp.int32), pick, side="right")
    return jax.random.permutation(jax.random.fold_in(stream_key, 2), count)[rank].astype(jnp.int32)


def scatter_about(rng, shape, spread, limit, pieces=(), dtype=jnp.bfloat16):
    gain = steps_of(rng, shape, pieces, -0.22, 0.18) if pieces else 1.0
    entries = jax.random.normal(rng, shape, jnp.float32) * spread * gain
    return jnp.minimum(jnp.maximum(entries, -limit), limit).astype(dtype)


def setup_inputs(seed: int = 0, part: int = 0) -> dict:
    key_of = jax.random.split(jax.random.key(seed), 8)
    part_keys = jax.random.split(jax.random.fold_in(key_of[7], part), 8)
    hidden = scatter_about(part_keys[0], (TOTAL_ROWS, HIDDEN_UNITS), 1.0, 6.0, ((0, 4), (1, 4)))
    frozen_down_weight = scatter_about(key_of[1], (HIDDEN_UNITS, MODEL_WIDTH), HIDDEN_UNITS ** -0.5, 0.03125, ((0, 4), (1, 4)))
    adapter_down_matrices = scatter_about(part_keys[2], (ADAPTER_JOBS, HIDDEN_UNITS, ADAPTER_RANK), HIDDEN_UNITS ** -0.5, 0.03125, ((0, 4), (1, 4)))
    adapter_up_matrices = scatter_about(part_keys[3], (ADAPTER_JOBS, ADAPTER_RANK, MODEL_WIDTH), ADAPTER_RANK ** -0.5, 0.75, ((0, 4), (2, 4)))
    row_block_job_ids = place_ends(ranked_ids(part_keys[4], (BLOCKS,), ADAPTER_JOBS, 2), jax.random.fold_in(part_keys[4], 3), 0, ADAPTER_JOBS - 1).astype(jnp.int32)
    home = jax.random.permutation(part_keys[5], ADAPTER_JOBS).astype(jnp.int32)
    cotangent = scatter_about(part_keys[6], (TOTAL_ROWS, MODEL_WIDTH), 1.0, 6.0, ((0, 4), (1, 4)))
    return dict(hidden=hidden, frozen_down_weight=frozen_down_weight, adapter_down_matrices=adapter_down_matrices, adapter_up_matrices=adapter_up_matrices, row_block_job_ids=row_block_job_ids, home=home, cotangent=cotangent)


adapter_scale = 2.0


def reference(hidden, frozen_down_weight, adapter_down_matrices, adapter_up_matrices, row_block_job_ids, home, cotangent):
    ff_group = HIDDEN_UNITS // N_TENSOR
    d_group = MODEL_WIDTH // N_JOB

    def add_group(index, running):
        offset = index * ff_group
        features = lax.dynamic_slice_in_dim(hidden, offset, ff_group, 1)
        weight_part = lax.dynamic_slice_in_dim(frozen_down_weight, offset, ff_group, 0)
        term = jnp.dot(features, weight_part, preferred_element_type=jnp.float32).astype(jnp.bfloat16)
        term = lax.optimization_barrier(term)
        return running + term.astype(jnp.float32)

    def back_group(index, running):
        offset = index * d_group
        columns = lax.dynamic_slice_in_dim(cotangent, offset, d_group, 1)
        weight_part = lax.dynamic_slice_in_dim(frozen_down_weight, offset, d_group, 1)
        term = lax.dot_general(columns, weight_part, (((1,), (1,)), ((), ())), preferred_element_type=jnp.float32).astype(jnp.bfloat16)
        term = lax.optimization_barrier(term)
        return running + term.astype(jnp.float32)

    frozen_output = lax.fori_loop(0, N_TENSOR, add_group, jnp.zeros((TOTAL_ROWS, MODEL_WIDTH), jnp.float32))
    frozen_backward = lax.fori_loop(0, N_JOB, back_group, jnp.zeros((TOTAL_ROWS, HIDDEN_UNITS), jnp.float32))
    storage_layout = jnp.take(home, row_block_job_ids).astype(jnp.int32)
    row_block_down_matrix = jnp.take(adapter_down_matrices, storage_layout, axis=0).astype(jnp.float32)
    row_block_up_matrix = jnp.take(adapter_up_matrices, storage_layout, axis=0).astype(jnp.float32)
    hid_blocks = hidden.reshape(BLOCKS, BLOCK, HIDDEN_UNITS).astype(jnp.float32)
    cotangent_row_blocks = cotangent.reshape(BLOCKS, BLOCK, MODEL_WIDTH).astype(jnp.float32)
    inner_low = jnp.einsum("nbf,nfr->nbr", hid_blocks, row_block_down_matrix).astype(jnp.bfloat16)
    inner_broad_product = inner_low.astype(jnp.float32)
    adapter_output = adapter_scale * jnp.einsum("xzh,xhk->xzk", inner_broad_product, row_block_up_matrix)
    mixed = (frozen_output + adapter_output.reshape(TOTAL_ROWS, MODEL_WIDTH)).astype(jnp.bfloat16)
    backward_narrow = (adapter_scale * jnp.einsum("cgx,csx->cgs", cotangent_row_blocks, row_block_up_matrix)).astype(jnp.bfloat16)
    backward_broad = backward_narrow.astype(jnp.float32)
    adapter_backward = jnp.einsum("cet,cqt->ceq", backward_broad, row_block_down_matrix).reshape(TOTAL_ROWS, HIDDEN_UNITS)
    hidden_gradient = (frozen_backward + adapter_backward).astype(jnp.bfloat16)
    up_gradient_terms = jnp.einsum("nbr,nbd->nrd", inner_broad_product, cotangent_row_blocks)
    down_terms = jnp.einsum("nbf,nbr->nfr", hid_blocks, backward_broad)
    up_matrix_gradient = (adapter_scale * jnp.zeros((ADAPTER_JOBS, ADAPTER_RANK, MODEL_WIDTH), jnp.float32).at[storage_layout].add(up_gradient_terms)).astype(jnp.bfloat16)
    grad_down = jnp.zeros((ADAPTER_JOBS, HIDDEN_UNITS, ADAPTER_RANK), jnp.float32).at[storage_layout].add(down_terms).astype(jnp.bfloat16)
    return (mixed, hidden_gradient, grad_down, up_matrix_gradient)
```

```python
import functools

import jax
import jax.numpy as jnp
from jax import lax
from jax.experimental import pallas as pl
from jax.experimental.pallas import tpu as pltpu
from jax.sharding import PartitionSpec as P

BLOCK = 128
RANK = 64
adapter_scale = 2.0
MESH = pl.DeviceIdType.MESH
F32 = jnp.float32
BF16 = jnp.bfloat16
NT = (((1,), (1,)), ((), ()))
TN = (((0,), (0,)), ((), ()))


def nn_dot(a, b):
    return jnp.dot(a, b, preferred_element_type=F32)


def nt_dot(a, b):
    return lax.dot_general(a, b, NT, preferred_element_type=F32)


def tn_dot(a, b):
    return lax.dot_general(a, b, TN, preferred_element_type=F32)


def fold_matrix(height):
    row = lax.broadcasted_iota(jnp.int32, (height, 2 * RANK), 0)
    lane = lax.broadcasted_iota(jnp.int32, (height, 2 * RANK), 1)
    return jnp.where(row % RANK == lane % RANK, 1.0, 0.0).astype(BF16)


def spread_matrix(first):
    row = lax.broadcasted_iota(jnp.int32, (2 * RANK, 2 * RANK), 0)
    lane = lax.broadcasted_iota(jnp.int32, (2 * RANK, 2 * RANK), 1)
    return jnp.where(row == lane % RANK + first, 1.0, 0.0).astype(BF16)


def step_kernel(
    T, J, ft, ct, chunks,
    hid, w, dn, up, mdn, mup, cot,
    mixed, hg, gd, ug,
    wv, hall, call, dnv, bpb, prv, xrv, fa, mst, mrv, ugv,
    backcat, innercat, pack, brt, brj, irt, irj,
    loc, c_s, c_r, hp_s, hp_r, ho_s, ho_r, hf_s, hf_r,
    b1_s, b1_r, b2_s, b2_r, i1_s, i1_r, i2_s, i2_r,
    ps, pr, xs, xr, ms, mr, outs,
):
    j = lax.axis_index("job")
    t = lax.axis_index("tensor")
    F, C = w.shape
    hr = hid.shape[0]
    cr = cot.shape[0]
    R = hr * J
    NP = J // 2
    nd = dn.shape[1] // RANK
    nu = up.shape[0] // RANK
    px = j // 2
    c = j % 2
    partner = 2 * px + 1 - c
    half = R // 2
    nft = F // ft
    nct = C // ct
    fch = F // chunks

    def remote(src, dst, s, r, axis, index):
        return pltpu.make_async_remote_copy(
            src_ref=src, dst_ref=dst, send_sem=s, recv_sem=r,
            device_id={axis: index}, device_id_type=MESH,
        )

    load_w = pltpu.make_async_copy(w, wv, loc.at[0])
    load_h = pltpu.make_async_copy(hid, hall.at[j], loc.at[1])
    load_c = pltpu.make_async_copy(cot, call.at[t], loc.at[2])
    load_d = pltpu.make_async_copy(dn, dnv, loc.at[3])
    load_h.start()
    load_w.start()
    load_c.start()
    load_d.start()

    barrier = pltpu.get_barrier_semaphore()
    for d in range(1, J):
        pl.semaphore_signal(barrier, inc=1, device_id={"job": (j + d) % J}, device_id_type=MESH)
    for d in range(1, T):
        pl.semaphore_signal(barrier, inc=1, device_id={"tensor": (t + d) % T}, device_id_type=MESH)
    pl.semaphore_wait(barrier, J + T - 2)

    sent = []
    outer = {}
    for ch in range(chunks):
        cols = pl.ds(ch * fch, fch)
        for d in range(1, NP):
            copy = remote(
                hid.at[:, cols], hall.at[j, :, cols],
                ho_s.at[d - 1, ch], ho_r.at[d - 1, ch], "job", (j + 2 * d) % J,
            )
            copy.start()
            outer[d, ch] = copy
            sent.append(copy)
    to_partner = remote(hid, hall.at[j], hp_s.at[0], hp_r.at[0], "job", partner)
    to_partner.start()
    sent.append(to_partner)
    cot_copies = []
    for d in range(1, T):
        copy = remote(cot, call.at[t], c_s.at[d - 1], c_r.at[d - 1], "tensor", (t + d) % T)
        copy.start()
        cot_copies.append(copy)
        sent.append(copy)

    load_h.wait()
    load_w.wait()
    to_partner.wait_recv()

    def columns(n):
        return pl.ds(pl.multiple_of(n * ct, ct), ct)

    @pl.loop(0, nct)
    def _(n):
        rows = hall[pl.ds(2 * px, 2)].reshape(2 * hr, F)
        fa[:, columns(n)] = nn_dot(rows, wv[:, columns(n)])

    forwards = []
    for ch in range(chunks):
        cols = pl.ds(ch * fch, fch)
        for d in range(1, NP):
            outer[d, ch].wait_recv()
            source = (j - 2 * d + J) % J
            part = hall.at[source, :, cols]
            copy = remote(part, part, hf_s.at[d - 1, ch], hf_r.at[d - 1, ch], "job", partner)
            copy.start()
            forwards.append(copy)
            sent.append(copy)

    lane_low = lax.broadcasted_iota(jnp.int32, (half, 2 * RANK), 1) < RANK

    def packed(masked, height):
        both = nn_dot(masked, fold_matrix(height))
        return jnp.where(lane_low, both[:half], both[half:]).astype(BF16)

    def send_all(src, land, s, r, axis, index, count):
        copies = []
        for d in range(1, count):
            copy = remote(src, land.at[d - 1], s.at[d - 1], r.at[d - 1], axis, (index + d) % count)
            copy.start()
            copies.append(copy)
            sent.append(copy)
        return copies

    def total_of(src, land, copies):
        total = src[...].astype(F32)
        for d, copy in enumerate(copies):
            copy.wait_recv()
            total = total + land[d].astype(F32)
        return total

    def spread(short, width):
        both = jnp.concatenate(
            [nn_dot(short, spread_matrix(0)), nn_dot(short, spread_matrix(RANK))], axis=0
        )
        return jnp.concatenate([both] * (width // 2), axis=1)

    load_c.wait()
    for copy in cot_copies:
        copy.wait_recv()
    part = nt_dot(call[...].reshape(R, C), up[...])
    pack[0] = packed((part * mup[...].astype(F32)).astype(BF16), nu * RANK)
    back_one = send_all(pack.at[0], brt, b1_s, b1_r, "tensor", t, T)

    load_d.wait()
    for copy in forwards:
        copy.wait_recv()

    @pl.loop(0, J)
    def _(b):
        rows = pl.ds(pl.multiple_of(b * hr, hr), hr)
        value = nn_dot(hall[b], dnv[...])
        backcat[rows] = (value * mdn[rows].astype(F32)).astype(BF16)

    pack[1] = packed(backcat[...], nd * RANK)
    inner_one = send_all(pack.at[1], irj, i1_s, i1_r, "job", j, J)
    pack[2] = total_of(pack.at[0], brt, back_one).astype(BF16)
    back_two = send_all(pack.at[2], brj, b2_s, b2_r, "job", j, J)
    pack[3] = total_of(pack.at[1], irj, inner_one).astype(BF16)
    inner_two = send_all(pack.at[3], irt, i2_s, i2_r, "tensor", t, T)
    back = (adapter_scale * total_of(pack.at[2], brj, back_two)).astype(BF16)
    backcat[...] = (spread(back, nd) * mdn[...].astype(F32)).astype(BF16)
    inner = total_of(pack.at[3], irt, inner_two).astype(BF16)
    innercat[...] = (adapter_scale * spread(inner, nu) * mup[...].astype(F32)).astype(BF16)

    blocks = 2 * hr // cr

    def mixed_copy(d):
        to = (t + d) % T
        return to, remote(mst.at[to], mrv.at[d - 1], ms.at[d - 1], mr.at[d - 1], "tensor", to)

    def pair_rows(pair):
        return pl.ds(pl.multiple_of(pair * 2 * hr, 2 * hr), 2 * hr)

    @pl.loop(0, nct)
    def _(n):
        value = fa[:, columns(n)] + nn_dot(innercat[pair_rows(px)], up[:, columns(n)])
        mst[pl.ds(px * blocks, blocks), :, columns(n)] = value.astype(BF16).reshape(blocks, cr, ct)

    for d in range(1, T):
        to, copy = mixed_copy(d)

        @pl.when(to // blocks == px)
        def _():
            copy.start()

    def tile(k):
        return pl.ds(pl.multiple_of(k * ft, ft), ft)

    def pair_copy(k):
        return remote(
            bpb.at[:, 1 - c, :, tile(k)], prv.at[:, :, tile(k)], ps.at[k], pr.at[k], "job", partner
        )

    def outer_copy(d, k):
        to = (j + 2 * d) % J
        return remote(
            bpb.at[to // 2, c, :, tile(k)], xrv.at[d - 1, :, tile(k)],
            xs.at[d - 1, k], xr.at[d - 1, k], "job", to,
        )

    def pass_on(k):
        pair_copy(k).wait_recv()
        both = bpb[:, c, :, tile(k)].astype(F32) + prv[:, :, tile(k)].astype(F32)
        bpb[:, c, :, tile(k)] = both.astype(BF16)
        for d in range(1, NP):
            outer_copy(d, k).start()

    @pl.loop(0, nft)
    def _(k):
        value = nt_dot(call[...].reshape(R, C), wv[tile(k)])
        value = value + nt_dot(backcat[...], dnv[tile(k)])
        bpb[:, :, :, tile(k)] = value.astype(BF16).reshape(NP, 2, hr, ft)
        pair_copy(k).start()
        grad = tn_dot(hall[:, :, tile(k)].reshape(R, ft), backcat[...])
        dnv[tile(k)] = grad.astype(BF16)

        @pl.when(k > 0)
        def _():
            pass_on(k - 1)

    pass_on(nft - 1)
    out_gd = pltpu.make_async_copy(dnv, gd, outs.at[0])
    out_gd.start()

    for e in range(1, NP):
        pair = (px + e) % NP

        @pl.loop(0, nct)
        def _(n):
            rows = hall[pl.ds(2 * pair, 2)].reshape(2 * hr, F)
            value = nn_dot(rows, wv[:, columns(n)])
            value = value + nn_dot(innercat[pair_rows(pair)], up[:, columns(n)])
            mst[pl.ds(pair * blocks, blocks), :, columns(n)] = value.astype(BF16).reshape(
                blocks, cr, ct
            )

        for d in range(1, T):
            to, copy = mixed_copy(d)

            @pl.when(to // blocks == pair)
            def _():
                copy.start()

    @pl.loop(0, nct)
    def _(n):
        cots = call[:, :, columns(n)].reshape(R, ct)
        ugv[:, columns(n)] = tn_dot(innercat[...], cots).astype(BF16)

    out_ug = pltpu.make_async_copy(ugv, ug, outs.at[1])
    out_ug.start()

    @pl.loop(0, nft)
    def _(k):
        value = bpb[px, c, :, tile(k)].astype(F32)
        for d in range(1, NP):
            outer_copy(d, k).wait_recv()
            value = value + xrv[d - 1, :, tile(k)].astype(F32)
        bpb[px, c, :, tile(k)] = value.astype(BF16)

    out_hg = pltpu.make_async_copy(bpb.at[px, c], hg, outs.at[2])
    out_hg.start()

    for d in range(1, T):
        mixed_copy(d)[1].wait_recv()

    @pl.loop(0, nct)
    def _(n):
        value = mst[t, :, columns(n)].astype(F32)
        for d in range(1, T):
            value = value + mrv[d - 1, :, columns(n)].astype(F32)
        mst[t, :, columns(n)] = value.astype(BF16)

    out_mx = pltpu.make_async_copy(mst.at[t], mixed, outs.at[3])
    out_mx.start()

    for copy in sent:
        copy.wait_send()
    for d in range(1, T):
        mixed_copy(d)[1].wait_send()

    @pl.loop(0, nft)
    def _(k):
        pair_copy(k).wait_send()
        for d in range(1, NP):
            outer_copy(d, k).wait_send()

    out_gd.wait()
    out_ug.wait()
    out_hg.wait()
    out_mx.wait()


def per_device(hidden, weight, downs, ups, block_jobs, home, cotangent):
    hr, F = hidden.shape
    cr, C = cotangent.shape
    T = lax.axis_size("tensor")
    J = lax.axis_size("job")
    R = hr * J
    NP = J // 2
    nd, nu = downs.shape[0], ups.shape[0]
    storage = jnp.repeat(jnp.take(home, block_jobs), BLOCK)[:, None]
    ndl, nul = nd * RANK, nu * RANK
    own_down = lax.axis_index("job") * nd + jnp.arange(ndl, dtype=jnp.int32)[None, :] // RANK
    own_up = lax.axis_index("tensor") * nu + jnp.arange(nul, dtype=jnp.int32)[None, :] // RANK
    mdn = (storage == own_down).astype(BF16)
    mup = (storage == own_up).astype(BF16)
    dn = jnp.transpose(downs, (1, 0, 2)).reshape(F, ndl)
    up = ups.reshape(nul, C)
    ft = 512 if F % 512 == 0 else 128
    ct = 256
    chunks = 4 if F % 512 == 0 else 1
    nft = F // ft
    sem = pltpu.SemaphoreType.DMA
    anyspace = pl.BlockSpec(memory_space=pl.ANY)
    vmem = pl.BlockSpec(memory_space=pltpu.VMEM)
    n_out = max(NP - 1, 1)
    mixed, hg, gd, ug = pl.pallas_call(
        functools.partial(step_kernel, T, J, ft, ct, chunks),
        out_shape=(
            jax.ShapeDtypeStruct((cr, C), BF16),
            jax.ShapeDtypeStruct((hr, F), BF16),
            jax.ShapeDtypeStruct((F, ndl), BF16),
            jax.ShapeDtypeStruct((nul, C), BF16),
        ),
        in_specs=[anyspace, anyspace, anyspace, vmem, vmem, vmem, anyspace],
        out_specs=(anyspace,) * 4,
        scratch_shapes=[
            pltpu.VMEM((F, C), BF16),
            pltpu.VMEM((J, hr, F), BF16),
            pltpu.VMEM((T, cr, C), BF16),
            pltpu.VMEM((F, ndl), BF16),
            pltpu.VMEM((NP, 2, hr, F), BF16),
            pltpu.VMEM((NP, hr, F), BF16),
            pltpu.VMEM((n_out, hr, F), BF16),
            pltpu.VMEM((2 * hr, C), F32),
            pltpu.VMEM((T, cr, C), BF16),
            pltpu.VMEM((T - 1, cr, C), BF16),
            pltpu.VMEM((nul, C), BF16),
            pltpu.VMEM((R, ndl), BF16),
            pltpu.VMEM((R, nul), BF16),
            pltpu.VMEM((4, R // 2, 2 * RANK), BF16),
            pltpu.VMEM((T - 1, R // 2, 2 * RANK), BF16),
            pltpu.VMEM((J - 1, R // 2, 2 * RANK), BF16),
            pltpu.VMEM((T - 1, R // 2, 2 * RANK), BF16),
            pltpu.VMEM((J - 1, R // 2, 2 * RANK), BF16),
            sem((4,)),
            sem((T - 1,)), sem((T - 1,)),
            sem((1,)), sem((1,)),
            sem((n_out, chunks)), sem((n_out, chunks)),
            sem((n_out, chunks)), sem((n_out, chunks)),
            sem((T - 1,)), sem((T - 1,)), sem((J - 1,)), sem((J - 1,)),
            sem((J - 1,)), sem((J - 1,)), sem((T - 1,)), sem((T - 1,)),
            sem((nft,)), sem((nft,)),
            sem((n_out, nft)), sem((n_out, nft)),
            sem((T - 1,)), sem((T - 1,)),
            sem((4,)),
        ],
        compiler_params=pltpu.CompilerParams(
            collective_id=0, has_side_effects=True, vmem_limit_bytes=64 * 1024 * 1024
        ),
    )(hidden, weight, dn, up, mdn, mup, cotangent)
    grad_down = jnp.transpose(gd.reshape(F, nd, RANK), (1, 0, 2))
    return mixed, hg, grad_down, ug.reshape(nu, RANK, C)


def solution(mesh):
    in_specs = (
        P(("group", "job"), "tensor"),
        P("tensor", "job"),
        P(("group", "job"), "tensor", None),
        P(("group", "tensor"), None, "job"),
        P("group"),
        P("group"),
        P(("group", "tensor"), "job"),
    )
    out_specs = (
        P(("group", "tensor"), "job"),
        P(("group", "job"), "tensor"),
        P(("group", "job"), "tensor", None),
        P(("group", "tensor"), None, "job"),
    )
    return jax.shard_map(
        per_device, mesh=mesh, in_specs=in_specs, out_specs=out_specs, check_vma=False
    )
```

```python
import functools

import jax
import jax.numpy as jnp
from jax import lax
from jax.experimental import pallas as pl
from jax.experimental.pallas import tpu as pltpu
from jax.sharding import PartitionSpec as P

BLOCK = 128
RANK = 64
adapter_scale = 2.0
MESH = pl.DeviceIdType.MESH
F32 = jnp.float32
BF16 = jnp.bfloat16
NT = (((1,), (1,)), ((), ()))
TN = (((0,), (0,)), ((), ()))


def nn_dot(a, b):
    return jnp.dot(a, b, preferred_element_type=F32)


def nt_dot(a, b):
    return lax.dot_general(a, b, NT, preferred_element_type=F32)


def tn_dot(a, b):
    return lax.dot_general(a, b, TN, preferred_element_type=F32)


def fold_matrix(height):
    row = lax.broadcasted_iota(jnp.int32, (height, 2 * RANK), 0)
    lane = lax.broadcasted_iota(jnp.int32, (height, 2 * RANK), 1)
    return jnp.where(row % RANK == lane % RANK, 1.0, 0.0).astype(BF16)


def spread_matrix(first):
    row = lax.broadcasted_iota(jnp.int32, (2 * RANK, 2 * RANK), 0)
    lane = lax.broadcasted_iota(jnp.int32, (2 * RANK, 2 * RANK), 1)
    return jnp.where(row == lane % RANK + first, 1.0, 0.0).astype(BF16)


def step_kernel(
    T, J, ft, ct, chunks,
    hid, w, dn, up, ids, home, cot,
    mixed, hg, gd, ug,
    wv, hall, call, dnv, bpb, prv, xrv, fa, mst, mrv, ugv,
    mdn, mup, backcat, innercat, pack, brt, brj, irt, irj,
    loc, c_s, c_r, hp_s, hp_r, ho_s, ho_r, hf_s, hf_r,
    b1_s, b1_r, b2_s, b2_r, i1_s, i1_r, i2_s, i2_r,
    ps, pr, xs, xr, ms, mr, outs,
):
    j = lax.axis_index("job")
    t = lax.axis_index("tensor")
    F, C = w.shape
    hr = hid.shape[0]
    cr = cot.shape[0]
    R = hr * J
    NP = J // 2
    nd = dn.shape[0] // RANK
    nu = up.shape[0] // RANK
    px = j // 2
    c = j % 2
    partner = 2 * px + 1 - c
    half = R // 2
    nft = F // ft
    nct = C // ct
    fch = F // chunks

    def remote(src, dst, s, r, axis, index):
        return pltpu.make_async_remote_copy(
            src_ref=src, dst_ref=dst, send_sem=s, recv_sem=r,
            device_id={axis: index}, device_id_type=MESH,
        )

    load_w = pltpu.make_async_copy(w, wv, loc.at[0])
    load_h = pltpu.make_async_copy(hid, hall.at[j], loc.at[1])
    load_c = pltpu.make_async_copy(cot, call.at[t], loc.at[2])
    load_d = pltpu.make_async_copy(dn, dnv, loc.at[3])
    load_h.start()
    load_w.start()
    load_c.start()
    load_d.start()

    for b in range(R // BLOCK):
        row = home[ids[b]]
        rows = slice(b * BLOCK, (b + 1) * BLOCK)
        for mask, first, count in ((mdn, j * nd, nd), (mup, t * nu, nu)):
            lane = lax.broadcasted_iota(jnp.int32, (BLOCK, count * RANK), 1)
            mask[rows] = jnp.where(lane // RANK + first == row, 1.0, 0.0).astype(BF16)

    barrier = pltpu.get_barrier_semaphore()
    for d in range(1, J):
        pl.semaphore_signal(barrier, inc=1, device_id={"job": (j + d) % J}, device_id_type=MESH)
    for d in range(1, T):
        pl.semaphore_signal(barrier, inc=1, device_id={"tensor": (t + d) % T}, device_id_type=MESH)
    pl.semaphore_wait(barrier, J + T - 2)

    sent = []
    outer = {}
    for ch in range(chunks):
        cols = pl.ds(ch * fch, fch)
        for d in range(1, NP):
            copy = remote(
                hid.at[:, cols], hall.at[j, :, cols],
                ho_s.at[d - 1, ch], ho_r.at[d - 1, ch], "job", (j + 2 * d) % J,
            )
            copy.start()
            outer[d, ch] = copy
            sent.append(copy)
    to_partner = remote(hid, hall.at[j], hp_s.at[0], hp_r.at[0], "job", partner)
    to_partner.start()
    sent.append(to_partner)

    def line_copy(step, up_way):
        block = t - step if up_way else t + step
        here = jnp.clip(block, 0, T - 1)
        src = cot if step == 0 else call.at[here]
        way = 0 if up_way else 1
        to = (t + 1) % T if up_way else (t + T - 1) % T
        copy = remote(src, call.at[here], c_s.at[way, step], c_r.at[way, step], "tensor", to)
        sends = ((block >= 0) & (t + 1 < T)) if up_way else ((block < T) & (t >= 1))
        lands = (t - 1 - step >= 0) if up_way else (t + 1 + step < T)
        return copy, sends, lands

    def line_each(step, act, landing):
        for up_way in (True, False):
            copy, sends, lands = line_copy(step, up_way)

            @pl.when(lands if landing else sends)
            def _():
                act(copy)

    def line_step(step):
        if step > 0:
            line_each(step - 1, lambda copy: copy.wait_recv(), True)
        if step < T - 1:
            line_each(step, lambda copy: copy.start(), False)

    forwards = []

    def forward(ch):
        cols = pl.ds(ch * fch, fch)
        for d in range(1, NP):
            outer[d, ch].wait_recv()
            source = (j - 2 * d + J) % J
            part = hall.at[source, :, cols]
            copy = remote(part, part, hf_s.at[d - 1, ch], hf_r.at[d - 1, ch], "job", partner)
            copy.start()
            forwards.append(copy)
            sent.append(copy)

    line_step(0)

    load_h.wait()
    load_w.wait()
    to_partner.wait_recv()

    def columns(n):
        return pl.ds(pl.multiple_of(n * ct, ct), ct)

    def own_forward(n):
        rows = hall[pl.ds(2 * px, 2)].reshape(2 * hr, F)
        fa[:, columns(n)] = nn_dot(rows, wv[:, columns(n)])

    early = min(2, chunks)
    forward(0)
    line_step(1)
    pl.loop(0, nct // 2)(own_forward)
    for ch in range(1, early):
        forward(ch)
    line_step(2)
    pl.loop(nct // 2, nct)(own_forward)
    for ch in range(early, chunks - 1):
        forward(ch)
    for step in range(3, T):
        line_step(step)

    lane_low = lax.broadcasted_iota(jnp.int32, (half, 2 * RANK), 1) < RANK

    def packed(masked, height):
        both = nn_dot(masked, fold_matrix(height))
        return jnp.where(lane_low, both[:half], both[half:]).astype(BF16)

    def send_all(src, land, s, r, axis, index, count):
        copies = []
        for d in range(1, count):
            copy = remote(src, land.at[d - 1], s.at[d - 1], r.at[d - 1], axis, (index + d) % count)
            copy.start()
            copies.append(copy)
            sent.append(copy)
        return copies

    def total_of(src, land, copies):
        total = src[...].astype(F32)
        for d, copy in enumerate(copies):
            copy.wait_recv()
            total = total + land[d].astype(F32)
        return total

    def spread(short, width):
        both = jnp.concatenate(
            [nn_dot(short, spread_matrix(0)), nn_dot(short, spread_matrix(RANK))], axis=0
        )
        return jnp.concatenate([both] * (width // 2), axis=1)

    load_c.wait()
    part = nt_dot(call[...].reshape(R, C), up[...])
    pack[0] = packed((part * mup[...].astype(F32)).astype(BF16), nu * RANK)
    back_one = send_all(pack.at[0], brt, b1_s, b1_r, "tensor", t, T)
    if chunks > early:
        forward(chunks - 1)
    pack[2] = total_of(pack.at[0], brt, back_one).astype(BF16)
    back_two = send_all(pack.at[2], brj, b2_s, b2_r, "job", j, J)

    load_d.wait()
    for copy in forwards:
        copy.wait_recv()

    @pl.loop(0, J)
    def _(b):
        rows = pl.ds(pl.multiple_of(b * hr, hr), hr)
        value = nt_dot(hall[b], dnv[...])
        backcat[rows] = (value * mdn[rows].astype(F32)).astype(BF16)

    pack[1] = packed(backcat[...], nd * RANK)
    inner_one = send_all(pack.at[1], irj, i1_s, i1_r, "job", j, J)
    back = (adapter_scale * total_of(pack.at[2], brj, back_two)).astype(BF16)
    backcat[...] = (spread(back, nd) * mdn[...].astype(F32)).astype(BF16)

    blocks = 2 * hr // cr

    def mixed_copy(d):
        to = (t + d) % T
        return to, remote(mst.at[to], mrv.at[d - 1], ms.at[d - 1], mr.at[d - 1], "tensor", to)

    def pair_rows(pair):
        return pl.ds(pl.multiple_of(pair * 2 * hr, 2 * hr), 2 * hr)

    def tile(k):
        return pl.ds(pl.multiple_of(k * ft, ft), ft)

    def pair_copy(k):
        return remote(
            bpb.at[:, 1 - c, :, tile(k)], prv.at[:, :, tile(k)], ps.at[k], pr.at[k], "job", partner
        )

    def outer_copy(d, k):
        to = (j + 2 * d) % J
        return remote(
            bpb.at[to // 2, c, :, tile(k)], xrv.at[d - 1, :, tile(k)],
            xs.at[d - 1, k], xr.at[d - 1, k], "job", to,
        )

    def pass_on(k):
        pair_copy(k).wait_recv()
        both = bpb[:, c, :, tile(k)].astype(F32) + prv[:, :, tile(k)].astype(F32)
        bpb[:, c, :, tile(k)] = both.astype(BF16)
        for d in range(1, NP):
            outer_copy(d, k).start()

    def backward(k):
        value = nt_dot(call[...].reshape(R, C), wv[tile(k)])
        value = value + nn_dot(backcat[...], dnv[:, tile(k)])
        bpb[:, :, :, tile(k)] = value.astype(BF16).reshape(NP, 2, hr, ft)
        pair_copy(k).start()
        grad = tn_dot(backcat[...], hall[:, :, tile(k)].reshape(R, ft))
        dnv[:, tile(k)] = grad.astype(BF16)

        @pl.when(k > 0)
        def _():
            pass_on(k - 1)

    def other_forward(n):
        for e in range(1, NP):
            pair = (px + e) % NP
            rows = hall[pl.ds(2 * pair, 2)].reshape(2 * hr, F)
            value = nn_dot(rows, wv[:, columns(n)])
            value = value + nn_dot(innercat[pair_rows(pair)], up[:, columns(n)])
            mst[pl.ds(pair * blocks, blocks), :, columns(n)] = value.astype(BF16).reshape(
                blocks, cr, ct
            )

    first = nft // 7
    second = 2 * first
    pl.loop(0, first)(backward)
    pack[3] = total_of(pack.at[1], irj, inner_one).astype(BF16)
    inner_two = send_all(pack.at[3], irt, i2_s, i2_r, "tensor", t, T)
    pl.loop(first, second)(backward)
    inner = total_of(pack.at[3], irt, inner_two).astype(BF16)
    innercat[...] = (adapter_scale * spread(inner, nu) * mup[...].astype(F32)).astype(BF16)

    @pl.loop(0, nct)
    def _(n):
        value = fa[:, columns(n)] + nn_dot(innercat[pair_rows(px)], up[:, columns(n)])
        mst[pl.ds(px * blocks, blocks), :, columns(n)] = value.astype(BF16).reshape(blocks, cr, ct)

    for d in range(1, T):
        to, copy = mixed_copy(d)

        @pl.when(to // blocks == px)
        def _():
            copy.start()

    third = second
    if nct <= nft - second:
        third = second + nct

        @pl.loop(0, nct)
        def _(n):
            other_forward(n)
            backward(second + n)
    else:
        pl.loop(0, nct)(other_forward)

    for d in range(1, T):
        to, copy = mixed_copy(d)

        @pl.when(to // blocks != px)
        def _():
            copy.start()

    pl.loop(third, nft)(backward)
    pass_on(nft - 1)
    out_gd = pltpu.make_async_copy(dnv, gd, outs.at[0])
    out_gd.start()

    @pl.loop(0, nct)
    def _(n):
        cots = call[:, :, columns(n)].reshape(R, ct)
        ugv[:, columns(n)] = tn_dot(innercat[...], cots).astype(BF16)

    out_ug = pltpu.make_async_copy(ugv, ug, outs.at[1])
    out_ug.start()

    @pl.loop(0, nft)
    def _(k):
        value = bpb[px, c, :, tile(k)].astype(F32)
        for d in range(1, NP):
            outer_copy(d, k).wait_recv()
            value = value + xrv[d - 1, :, tile(k)].astype(F32)
        bpb[px, c, :, tile(k)] = value.astype(BF16)

    out_hg = pltpu.make_async_copy(bpb.at[px, c], hg, outs.at[2])
    out_hg.start()

    for d in range(1, T):
        mixed_copy(d)[1].wait_recv()

    @pl.loop(0, nct)
    def _(n):
        value = mst[t, :, columns(n)].astype(F32)
        for d in range(1, T):
            value = value + mrv[d - 1, :, columns(n)].astype(F32)
        mst[t, :, columns(n)] = value.astype(BF16)

    out_mx = pltpu.make_async_copy(mst.at[t], mixed, outs.at[3])
    out_mx.start()

    for copy in sent:
        copy.wait_send()
    for step in range(T - 1):
        line_each(step, lambda copy: copy.wait_send(), False)
    for d in range(1, T):
        mixed_copy(d)[1].wait_send()

    @pl.loop(0, nft)
    def _(k):
        pair_copy(k).wait_send()
        for d in range(1, NP):
            outer_copy(d, k).wait_send()

    out_gd.wait()
    out_ug.wait()
    out_hg.wait()
    out_mx.wait()


def per_device(hidden, weight, downs, ups, block_jobs, home, cotangent):
    hr, F = hidden.shape
    cr, C = cotangent.shape
    T = lax.axis_size("tensor")
    J = lax.axis_size("job")
    R = hr * J
    NP = J // 2
    nd, nu = downs.shape[0], ups.shape[0]
    ndl, nul = nd * RANK, nu * RANK
    dn = jnp.transpose(downs, (0, 2, 1)).reshape(ndl, F)
    up = ups.reshape(nul, C)
    ft = 512 if F % 512 == 0 else 128
    ct = 256
    chunks = 4 if F % 512 == 0 else 1
    nft = F // ft
    sem = pltpu.SemaphoreType.DMA
    anyspace = pl.BlockSpec(memory_space=pl.ANY)
    smem = pl.BlockSpec(memory_space=pltpu.SMEM)
    vmem = pl.BlockSpec(memory_space=pltpu.VMEM)
    n_out = max(NP - 1, 1)
    mixed, hg, gd, ug = pl.pallas_call(
        functools.partial(step_kernel, T, J, ft, ct, chunks),
        out_shape=(
            jax.ShapeDtypeStruct((cr, C), BF16),
            jax.ShapeDtypeStruct((hr, F), BF16),
            jax.ShapeDtypeStruct((ndl, F), BF16),
            jax.ShapeDtypeStruct((nul, C), BF16),
        ),
        in_specs=[anyspace, anyspace, anyspace, vmem, smem, smem, anyspace],
        out_specs=(anyspace,) * 4,
        scratch_shapes=[
            pltpu.VMEM((F, C), BF16),
            pltpu.VMEM((J, hr, F), BF16),
            pltpu.VMEM((T, cr, C), BF16),
            pltpu.VMEM((ndl, F), BF16),
            pltpu.VMEM((NP, 2, hr, F), BF16),
            pltpu.VMEM((NP, hr, F), BF16),
            pltpu.VMEM((n_out, hr, F), BF16),
            pltpu.VMEM((2 * hr, C), F32),
            pltpu.VMEM((T, cr, C), BF16),
            pltpu.VMEM((T - 1, cr, C), BF16),
            pltpu.VMEM((nul, C), BF16),
            pltpu.VMEM((R, ndl), BF16),
            pltpu.VMEM((R, nul), BF16),
            pltpu.VMEM((R, ndl), BF16),
            pltpu.VMEM((R, nul), BF16),
            pltpu.VMEM((4, R // 2, 2 * RANK), BF16),
            pltpu.VMEM((T - 1, R // 2, 2 * RANK), BF16),
            pltpu.VMEM((J - 1, R // 2, 2 * RANK), BF16),
            pltpu.VMEM((T - 1, R // 2, 2 * RANK), BF16),
            pltpu.VMEM((J - 1, R // 2, 2 * RANK), BF16),
            sem((4,)),
            sem((2, T - 1)), sem((2, T - 1)),
            sem((1,)), sem((1,)),
            sem((n_out, chunks)), sem((n_out, chunks)),
            sem((n_out, chunks)), sem((n_out, chunks)),
            sem((T - 1,)), sem((T - 1,)), sem((J - 1,)), sem((J - 1,)),
            sem((J - 1,)), sem((J - 1,)), sem((T - 1,)), sem((T - 1,)),
            sem((nft,)), sem((nft,)),
            sem((n_out, nft)), sem((n_out, nft)),
            sem((T - 1,)), sem((T - 1,)),
            sem((4,)),
        ],
        compiler_params=pltpu.CompilerParams(
            collective_id=0, has_side_effects=True, vmem_limit_bytes=64 * 1024 * 1024
        ),
    )(hidden, weight, dn, up, block_jobs, home, cotangent)
    grad_down = jnp.transpose(gd.reshape(nd, RANK, F), (0, 2, 1))
    return mixed, hg, grad_down, ug.reshape(nu, RANK, C)


def solution(mesh):
    in_specs = (
        P(("group", "job"), "tensor"),
        P("tensor", "job"),
        P(("group", "job"), "tensor", None),
        P(("group", "tensor"), None, "job"),
        P("group"),
        P("group"),
        P(("group", "tensor"), "job"),
    )
    out_specs = (
        P(("group", "tensor"), "job"),
        P(("group", "job"), "tensor"),
        P(("group", "job"), "tensor", None),
        P(("group", "tensor"), None, "job"),
    )
    return jax.shard_map(
        per_device, mesh=mesh, in_specs=in_specs, out_specs=out_specs, check_vma=False
    )
```

```python
import functools

import jax
import jax.numpy as jnp
from jax import lax
from jax.experimental import pallas as pl
from jax.experimental.pallas import tpu as pltpu
from jax.sharding import PartitionSpec as P

BLOCK = 128
RANK = 64
adapter_scale = 2.0
MESH = pl.DeviceIdType.MESH
F32 = jnp.float32
BF16 = jnp.bfloat16
NT = (((1,), (1,)), ((), ()))
TN = (((0,), (0,)), ((), ()))


def nn_dot(a, b):
    return jnp.dot(a, b, preferred_element_type=F32)


def nt_dot(a, b):
    return lax.dot_general(a, b, NT, preferred_element_type=F32)


def tn_dot(a, b):
    return lax.dot_general(a, b, TN, preferred_element_type=F32)


def fold_matrix(height):
    row = lax.broadcasted_iota(jnp.int32, (height, 2 * RANK), 0)
    lane = lax.broadcasted_iota(jnp.int32, (height, 2 * RANK), 1)
    return jnp.where(row % RANK == lane % RANK, 1.0, 0.0).astype(BF16)


def spread_matrix(first):
    row = lax.broadcasted_iota(jnp.int32, (2 * RANK, 2 * RANK), 0)
    lane = lax.broadcasted_iota(jnp.int32, (2 * RANK, 2 * RANK), 1)
    return jnp.where(row == lane % RANK + first, 1.0, 0.0).astype(BF16)


def step_kernel(
    T, J, ft, ct, chunks,
    hid, w, dn, up, ids, home, cot,
    mixed, hg, gd, ug,
    wv, hall, call, dnv, bpb, prv, xrv, fa, mst, mrv, ugv,
    mdn, mup, backcat, innercat, pack, brt, brj, irt, irj,
    loc, c_s, c_r, hp_s, hp_r, ho_s, ho_r, hf_s, hf_r,
    b1_s, b1_r, b2_s, b2_r, i1_s, i1_r, i2_s, i2_r,
    ps, pr, xs, xr, ms, mr, outs,
):
    j = lax.axis_index("job")
    t = lax.axis_index("tensor")
    F, C = w.shape
    hr = hid.shape[0]
    cr = cot.shape[0]
    R = hr * J
    NP = J // 2
    nd = dn.shape[0] // RANK
    nu = up.shape[0] // RANK
    px = j // 2
    c = j % 2
    partner = 2 * px + 1 - c
    half = R // 2
    nft = F // ft
    nct = C // ct
    fch = F // chunks

    def remote(src, dst, s, r, axis, index):
        return pltpu.make_async_remote_copy(
            src_ref=src, dst_ref=dst, send_sem=s, recv_sem=r,
            device_id={axis: index}, device_id_type=MESH,
        )

    load_w = pltpu.make_async_copy(w, wv, loc.at[0])
    load_h = pltpu.make_async_copy(hid, hall.at[j], loc.at[1])
    load_c = pltpu.make_async_copy(cot, call.at[t], loc.at[2])
    load_d = pltpu.make_async_copy(dn, dnv, loc.at[3])
    load_h.start()
    load_w.start()
    load_c.start()
    load_d.start()

    for b in range(R // BLOCK):
        row = home[ids[b]]
        rows = slice(b * BLOCK, (b + 1) * BLOCK)
        for mask, first, count in ((mdn, j * nd, nd), (mup, t * nu, nu)):
            lane = lax.broadcasted_iota(jnp.int32, (BLOCK, count * RANK), 1)
            mask[rows] = jnp.where(lane // RANK + first == row, 1.0, 0.0).astype(BF16)

    barrier = pltpu.get_barrier_semaphore()
    for d in range(1, J):
        pl.semaphore_signal(barrier, inc=1, device_id={"job": (j + d) % J}, device_id_type=MESH)
    for d in range(1, T):
        pl.semaphore_signal(barrier, inc=1, device_id={"tensor": (t + d) % T}, device_id_type=MESH)
    pl.semaphore_wait(barrier, J + T - 2)

    sent = []
    outer = {}
    for ch in range(chunks):
        cols = pl.ds(ch * fch, fch)
        for d in range(1, NP):
            copy = remote(
                hid.at[:, cols], hall.at[j, :, cols],
                ho_s.at[d - 1, ch], ho_r.at[d - 1, ch], "job", (j + 2 * d) % J,
            )
            copy.start()
            outer[d, ch] = copy
            sent.append(copy)
    to_partner = remote(hid, hall.at[j], hp_s.at[0], hp_r.at[0], "job", partner)
    to_partner.start()
    sent.append(to_partner)

    def line_copy(step, up_way):
        block = t - step if up_way else t + step
        here = jnp.clip(block, 0, T - 1)
        src = cot if step == 0 else call.at[here]
        way = 0 if up_way else 1
        to = (t + 1) % T if up_way else (t + T - 1) % T
        copy = remote(src, call.at[here], c_s.at[way, step], c_r.at[way, step], "tensor", to)
        sends = ((block >= 0) & (t + 1 < T)) if up_way else ((block < T) & (t >= 1))
        lands = (t - 1 - step >= 0) if up_way else (t + 1 + step < T)
        return copy, sends, lands

    def line_each(step, act, landing):
        for up_way in (True, False):
            copy, sends, lands = line_copy(step, up_way)

            @pl.when(lands if landing else sends)
            def _():
                act(copy)

    def line_step(step):
        if step > 0:
            line_each(step - 1, lambda copy: copy.wait_recv(), True)
        if step < T - 1:
            line_each(step, lambda copy: copy.start(), False)

    forwards = []

    def forward(ch):
        cols = pl.ds(ch * fch, fch)
        for d in range(1, NP):
            outer[d, ch].wait_recv()
            source = (j - 2 * d + J) % J
            part = hall.at[source, :, cols]
            copy = remote(part, part, hf_s.at[d - 1, ch], hf_r.at[d - 1, ch], "job", partner)
            copy.start()
            forwards.append(copy)
            sent.append(copy)

    line_step(0)

    load_h.wait()
    load_w.wait()
    to_partner.wait_recv()

    def columns(n):
        return pl.ds(pl.multiple_of(n * ct, ct), ct)

    def own_forward(n):
        rows = hall[pl.ds(2 * px, 2)].reshape(2 * hr, F)
        fa[:, columns(n)] = nn_dot(rows, wv[:, columns(n)])

    early = min(2, chunks)
    forward(0)
    line_step(1)
    pl.loop(0, nct // 2)(own_forward)
    for ch in range(1, early):
        forward(ch)
    line_step(2)
    pl.loop(nct // 2, nct)(own_forward)
    for ch in range(early, chunks - 1):
        forward(ch)
    for step in range(3, T):
        line_step(step)

    lane_low = lax.broadcasted_iota(jnp.int32, (half, 2 * RANK), 1) < RANK

    def packed(masked, height):
        both = nn_dot(masked, fold_matrix(height))
        return jnp.where(lane_low, both[:half], both[half:]).astype(BF16)

    def send_all(src, land, s, r, axis, index, count):
        copies = []
        for d in range(1, count):
            copy = remote(src, land.at[d - 1], s.at[d - 1], r.at[d - 1], axis, (index + d) % count)
            copy.start()
            copies.append(copy)
            sent.append(copy)
        return copies

    def total_of(src, land, copies):
        total = src[...].astype(F32)
        for d, copy in enumerate(copies):
            copy.wait_recv()
            total = total + land[d].astype(F32)
        return total

    def spread(short, width):
        both = jnp.concatenate(
            [nn_dot(short, spread_matrix(0)), nn_dot(short, spread_matrix(RANK))], axis=0
        )
        return jnp.concatenate([both] * (width // 2), axis=1)

    load_c.wait()
    part = nt_dot(call[...].reshape(R, C), up[...])
    pack[0] = packed((part * mup[...].astype(F32)).astype(BF16), nu * RANK)
    back_one = send_all(pack.at[0], brt, b1_s, b1_r, "tensor", t, T)
    if chunks > early:
        forward(chunks - 1)
    pack[2] = total_of(pack.at[0], brt, back_one).astype(BF16)
    back_two = send_all(pack.at[2], brj, b2_s, b2_r, "job", j, J)

    load_d.wait()
    for copy in forwards:
        copy.wait_recv()

    @pl.loop(0, J)
    def _(b):
        rows = pl.ds(pl.multiple_of(b * hr, hr), hr)
        value = nt_dot(hall[b], dnv[...])
        backcat[rows] = (value * mdn[rows].astype(F32)).astype(BF16)

    pack[1] = packed(backcat[...], nd * RANK)
    inner_one = send_all(pack.at[1], irj, i1_s, i1_r, "job", j, J)
    back = (adapter_scale * total_of(pack.at[2], brj, back_two)).astype(BF16)
    backcat[...] = (spread(back, nd) * mdn[...].astype(F32)).astype(BF16)

    blocks = 2 * hr // cr

    def mixed_copy(d, h):
        to = (t + d) % T
        cols = pl.ds(h * (C // 2), C // 2)
        return to, remote(
            mst.at[to, :, cols], mrv.at[d - 1, :, cols],
            ms.at[d - 1, h], mr.at[d - 1, h], "tensor", to,
        )

    def send_mixed(own, h):
        for d in range(1, T):
            to, copy = mixed_copy(d, h)

            @pl.when((to // blocks == px) if own else (to // blocks != px))
            def _():
                copy.start()

    def pair_rows(pair):
        return pl.ds(pl.multiple_of(pair * 2 * hr, 2 * hr), 2 * hr)

    def tile(k):
        return pl.ds(pl.multiple_of(k * ft, ft), ft)

    def pair_copy(k):
        return remote(
            bpb.at[:, 1 - c, :, tile(k)], prv.at[:, :, tile(k)], ps.at[k], pr.at[k], "job", partner
        )

    def outer_copy(d, k):
        to = (j + 2 * d) % J
        return remote(
            bpb.at[to // 2, c, :, tile(k)], xrv.at[d - 1, :, tile(k)],
            xs.at[d - 1, k], xr.at[d - 1, k], "job", to,
        )

    def pass_on(k):
        pair_copy(k).wait_recv()
        both = bpb[:, c, :, tile(k)].astype(F32) + prv[:, :, tile(k)].astype(F32)
        bpb[:, c, :, tile(k)] = both.astype(BF16)
        for d in range(1, NP):
            outer_copy(d, k).start()

    def backward(k):
        value = nt_dot(call[...].reshape(R, C), wv[tile(k)])
        value = value + nn_dot(backcat[...], dnv[:, tile(k)])
        bpb[:, :, :, tile(k)] = value.astype(BF16).reshape(NP, 2, hr, ft)
        pair_copy(k).start()
        grad = tn_dot(backcat[...], hall[:, :, tile(k)].reshape(R, ft))
        dnv[:, tile(k)] = grad.astype(BF16)

        @pl.when(k > 0)
        def _():
            pass_on(k - 1)

    def other_forward(n):
        for e in range(1, NP):
            pair = (px + e) % NP
            rows = hall[pl.ds(2 * pair, 2)].reshape(2 * hr, F)
            value = nn_dot(rows, wv[:, columns(n)])
            value = value + nn_dot(innercat[pair_rows(pair)], up[:, columns(n)])
            mst[pl.ds(pair * blocks, blocks), :, columns(n)] = value.astype(BF16).reshape(
                blocks, cr, ct
            )

    first = max(1, nft // 14)
    second = 2 * first
    pl.loop(0, first)(backward)
    pack[3] = total_of(pack.at[1], irj, inner_one).astype(BF16)
    inner_two = send_all(pack.at[3], irt, i2_s, i2_r, "tensor", t, T)
    pl.loop(first, second)(backward)
    inner = total_of(pack.at[3], irt, inner_two).astype(BF16)
    innercat[...] = (adapter_scale * spread(inner, nu) * mup[...].astype(F32)).astype(BF16)

    @pl.loop(0, nct)
    def _(n):
        value = fa[:, columns(n)] + nn_dot(innercat[pair_rows(px)], up[:, columns(n)])
        mst[pl.ds(px * blocks, blocks), :, columns(n)] = value.astype(BF16).reshape(blocks, cr, ct)

    send_mixed(True, 0)
    send_mixed(True, 1)

    beside = nct <= nft - second

    def joint(n):
        other_forward(n)
        if beside:
            backward(second + n)

    pl.loop(0, nct // 2)(joint)
    send_mixed(False, 0)
    pl.loop(nct // 2, nct)(joint)
    send_mixed(False, 1)
    third = second + nct if beside else second
    pl.loop(third, nft)(backward)
    pass_on(nft - 1)
    out_gd = pltpu.make_async_copy(dnv, gd, outs.at[0])
    out_gd.start()

    @pl.loop(0, nct)
    def _(n):
        cots = call[:, :, columns(n)].reshape(R, ct)
        ugv[:, columns(n)] = tn_dot(innercat[...], cots).astype(BF16)

    out_ug = pltpu.make_async_copy(ugv, ug, outs.at[1])
    out_ug.start()

    @pl.loop(0, nft)
    def _(k):
        value = bpb[px, c, :, tile(k)].astype(F32)
        for d in range(1, NP):
            outer_copy(d, k).wait_recv()
            value = value + xrv[d - 1, :, tile(k)].astype(F32)
        bpb[px, c, :, tile(k)] = value.astype(BF16)

    out_hg = pltpu.make_async_copy(bpb.at[px, c], hg, outs.at[2])
    out_hg.start()

    for h in range(2):
        for d in range(1, T):
            mixed_copy(d, h)[1].wait_recv()

        @pl.loop(h * (nct // 2), (h + 1) * (nct // 2))
        def _(n):
            value = mst[t, :, columns(n)].astype(F32)
            for d in range(1, T):
                value = value + mrv[d - 1, :, columns(n)].astype(F32)
            mst[t, :, columns(n)] = value.astype(BF16)

    out_mx = pltpu.make_async_copy(mst.at[t], mixed, outs.at[3])
    out_mx.start()

    for copy in sent:
        copy.wait_send()
    for step in range(T - 1):
        line_each(step, lambda copy: copy.wait_send(), False)
    for h in range(2):
        for d in range(1, T):
            mixed_copy(d, h)[1].wait_send()

    @pl.loop(0, nft)
    def _(k):
        pair_copy(k).wait_send()
        for d in range(1, NP):
            outer_copy(d, k).wait_send()

    out_gd.wait()
    out_ug.wait()
    out_hg.wait()
    out_mx.wait()


def per_device(hidden, weight, downs, ups, block_jobs, home, cotangent):
    hr, F = hidden.shape
    cr, C = cotangent.shape
    T = lax.axis_size("tensor")
    J = lax.axis_size("job")
    R = hr * J
    NP = J // 2
    nd, nu = downs.shape[0], ups.shape[0]
    ndl, nul = nd * RANK, nu * RANK
    dn = jnp.transpose(downs, (0, 2, 1)).reshape(ndl, F)
    up = ups.reshape(nul, C)
    ft = 512 if F % 512 == 0 else 128
    ct = 256
    chunks = 4 if F % 512 == 0 else 1
    nft = F // ft
    sem = pltpu.SemaphoreType.DMA
    anyspace = pl.BlockSpec(memory_space=pl.ANY)
    smem = pl.BlockSpec(memory_space=pltpu.SMEM)
    vmem = pl.BlockSpec(memory_space=pltpu.VMEM)
    n_out = max(NP - 1, 1)
    mixed, hg, gd, ug = pl.pallas_call(
        functools.partial(step_kernel, T, J, ft, ct, chunks),
        out_shape=(
            jax.ShapeDtypeStruct((cr, C), BF16),
            jax.ShapeDtypeStruct((hr, F), BF16),
            jax.ShapeDtypeStruct((ndl, F), BF16),
            jax.ShapeDtypeStruct((nul, C), BF16),
        ),
        in_specs=[anyspace, anyspace, anyspace, vmem, smem, smem, anyspace],
        out_specs=(anyspace,) * 4,
        scratch_shapes=[
            pltpu.VMEM((F, C), BF16),
            pltpu.VMEM((J, hr, F), BF16),
            pltpu.VMEM((T, cr, C), BF16),
            pltpu.VMEM((ndl, F), BF16),
            pltpu.VMEM((NP, 2, hr, F), BF16),
            pltpu.VMEM((NP, hr, F), BF16),
            pltpu.VMEM((n_out, hr, F), BF16),
            pltpu.VMEM((2 * hr, C), F32),
            pltpu.VMEM((T, cr, C), BF16),
            pltpu.VMEM((T - 1, cr, C), BF16),
            pltpu.VMEM((nul, C), BF16),
            pltpu.VMEM((R, ndl), BF16),
            pltpu.VMEM((R, nul), BF16),
            pltpu.VMEM((R, ndl), BF16),
            pltpu.VMEM((R, nul), BF16),
            pltpu.VMEM((4, R // 2, 2 * RANK), BF16),
            pltpu.VMEM((T - 1, R // 2, 2 * RANK), BF16),
            pltpu.VMEM((J - 1, R // 2, 2 * RANK), BF16),
            pltpu.VMEM((T - 1, R // 2, 2 * RANK), BF16),
            pltpu.VMEM((J - 1, R // 2, 2 * RANK), BF16),
            sem((4,)),
            sem((2, T - 1)), sem((2, T - 1)),
            sem((1,)), sem((1,)),
            sem((n_out, chunks)), sem((n_out, chunks)),
            sem((n_out, chunks)), sem((n_out, chunks)),
            sem((T - 1,)), sem((T - 1,)), sem((J - 1,)), sem((J - 1,)),
            sem((J - 1,)), sem((J - 1,)), sem((T - 1,)), sem((T - 1,)),
            sem((nft,)), sem((nft,)),
            sem((n_out, nft)), sem((n_out, nft)),
            sem((T - 1, 2)), sem((T - 1, 2)),
            sem((4,)),
        ],
        compiler_params=pltpu.CompilerParams(
            collective_id=0, has_side_effects=True, vmem_limit_bytes=64 * 1024 * 1024
        ),
    )(hidden, weight, dn, up, block_jobs, home, cotangent)
    grad_down = jnp.transpose(gd.reshape(nd, RANK, F), (0, 2, 1))
    return mixed, hg, grad_down, ug.reshape(nu, RANK, C)


def solution(mesh):
    in_specs = (
        P(("group", "job"), "tensor"),
        P("tensor", "job"),
        P(("group", "job"), "tensor", None),
        P(("group", "tensor"), None, "job"),
        P("group"),
        P("group"),
        P(("group", "tensor"), "job"),
    )
    out_specs = (
        P(("group", "tensor"), "job"),
        P(("group", "job"), "tensor"),
        P(("group", "job"), "tensor", None),
        P(("group", "tensor"), None, "job"),
    )
    return jax.shard_map(
        per_device, mesh=mesh, in_specs=in_specs, out_specs=out_specs, check_vma=False
    )
```

```python
import functools

import jax
import jax.numpy as jnp
from jax import lax
from jax.experimental import pallas as pl
from jax.experimental.pallas import tpu as pltpu
from jax.sharding import PartitionSpec as P

BLOCK = 128
RANK = 64
adapter_scale = 2.0
MESH = pl.DeviceIdType.MESH
F32 = jnp.float32
BF16 = jnp.bfloat16
NT = (((1,), (1,)), ((), ()))
TN = (((0,), (0,)), ((), ()))


def nn_dot(a, b):
    return jnp.dot(a, b, preferred_element_type=F32)


def nt_dot(a, b):
    return lax.dot_general(a, b, NT, preferred_element_type=F32)


def tn_dot(a, b):
    return lax.dot_general(a, b, TN, preferred_element_type=F32)


def fold_matrix(height):
    row = lax.broadcasted_iota(jnp.int32, (height, 2 * RANK), 0)
    lane = lax.broadcasted_iota(jnp.int32, (height, 2 * RANK), 1)
    return jnp.where(row % RANK == lane % RANK, 1.0, 0.0).astype(BF16)


def spread_matrix(first):
    row = lax.broadcasted_iota(jnp.int32, (2 * RANK, 2 * RANK), 0)
    lane = lax.broadcasted_iota(jnp.int32, (2 * RANK, 2 * RANK), 1)
    return jnp.where(row == lane % RANK + first, 1.0, 0.0).astype(BF16)


def step_kernel(
    T, J, ft, ct, chunks,
    hid, w, dn, up, ids, home, cot,
    mixed, hg, gd, ug,
    wv, hall, call, dnv, bpb, prv, xrv, fa, mst, mrv, ugv,
    mdn, mup, backcat, innercat, pack, brt, brj, irt, irj,
    loc, c_s, c_r, hp_s, hp_r, ho_s, ho_r, hf_s, hf_r,
    b1_s, b1_r, b2_s, b2_r, i1_s, i1_r, i2_s, i2_r,
    ps, pr, xs, xr, ms, mr, outs,
):
    j = lax.axis_index("job")
    t = lax.axis_index("tensor")
    F, C = w.shape
    hr = hid.shape[0]
    cr = cot.shape[0]
    R = hr * J
    NP = J // 2
    nd = dn.shape[0] // RANK
    nu = up.shape[0] // RANK
    px = j // 2
    c = j % 2
    partner = 2 * px + 1 - c
    half = R // 2
    nft = F // ft
    nct = C // ct
    fch = F // chunks

    def remote(src, dst, s, r, axis, index):
        return pltpu.make_async_remote_copy(
            src_ref=src, dst_ref=dst, send_sem=s, recv_sem=r,
            device_id={axis: index}, device_id_type=MESH,
        )

    load_w = pltpu.make_async_copy(w, wv, loc.at[0])
    load_h = pltpu.make_async_copy(hid, hall.at[j], loc.at[1])
    load_c = pltpu.make_async_copy(cot, call.at[t], loc.at[2])
    load_d = pltpu.make_async_copy(dn, dnv, loc.at[3])
    load_h.start()
    load_w.start()
    load_c.start()
    load_d.start()

    for b in range(R // BLOCK):
        row = home[ids[b]]
        rows = slice(b * BLOCK, (b + 1) * BLOCK)
        for mask, first, count in ((mdn, j * nd, nd), (mup, t * nu, nu)):
            lane = lax.broadcasted_iota(jnp.int32, (BLOCK, count * RANK), 1)
            mask[rows] = jnp.where(lane // RANK + first == row, 1.0, 0.0).astype(BF16)

    barrier = pltpu.get_barrier_semaphore()
    for d in range(1, J):
        pl.semaphore_signal(barrier, inc=1, device_id={"job": (j + d) % J}, device_id_type=MESH)
    for d in range(1, T):
        pl.semaphore_signal(barrier, inc=1, device_id={"tensor": (t + d) % T}, device_id_type=MESH)
    pl.semaphore_wait(barrier, J + T - 2)

    sent = []
    outer = {}
    for ch in range(chunks):
        cols = pl.ds(ch * fch, fch)
        for d in range(1, NP):
            copy = remote(
                hid.at[:, cols], hall.at[j, :, cols],
                ho_s.at[d - 1, ch], ho_r.at[d - 1, ch], "job", (j + 2 * d) % J,
            )
            copy.start()
            outer[d, ch] = copy
            sent.append(copy)
    to_partner = remote(hid, hall.at[j], hp_s.at[0], hp_r.at[0], "job", partner)
    to_partner.start()
    sent.append(to_partner)

    def line_copy(step, up_way):
        block = t - step if up_way else t + step
        here = jnp.clip(block, 0, T - 1)
        src = cot if step == 0 else call.at[here]
        way = 0 if up_way else 1
        to = (t + 1) % T if up_way else (t + T - 1) % T
        copy = remote(src, call.at[here], c_s.at[way, step], c_r.at[way, step], "tensor", to)
        sends = ((block >= 0) & (t + 1 < T)) if up_way else ((block < T) & (t >= 1))
        lands = (t - 1 - step >= 0) if up_way else (t + 1 + step < T)
        return copy, sends, lands

    def line_each(step, act, landing):
        for up_way in (True, False):
            copy, sends, lands = line_copy(step, up_way)

            @pl.when(lands if landing else sends)
            def _():
                act(copy)

    def line_step(step):
        if step > 0:
            line_each(step - 1, lambda copy: copy.wait_recv(), True)
        if step < T - 1:
            line_each(step, lambda copy: copy.start(), False)

    forwards = []

    def forward(ch):
        cols = pl.ds(ch * fch, fch)
        for d in range(1, NP):
            outer[d, ch].wait_recv()
            source = (j - 2 * d + J) % J
            part = hall.at[source, :, cols]
            copy = remote(part, part, hf_s.at[d - 1, ch], hf_r.at[d - 1, ch], "job", partner)
            copy.start()
            forwards.append(copy)
            sent.append(copy)

    line_step(0)

    load_h.wait()
    load_w.wait()
    to_partner.wait_recv()

    def columns(n):
        return pl.ds(pl.multiple_of(n * ct, ct), ct)

    def own_forward(n):
        rows = hall[pl.ds(2 * px, 2)].reshape(2 * hr, F)
        fa[:, columns(n)] = nn_dot(rows, wv[:, columns(n)])

    early = min(2, chunks)
    forward(0)
    line_step(1)
    pl.loop(0, nct // 2)(own_forward)
    for ch in range(1, early):
        forward(ch)
    line_step(2)
    pl.loop(nct // 2, nct)(own_forward)
    for ch in range(early, chunks - 1):
        forward(ch)
    for step in range(3, T):
        line_step(step)

    lane_low = lax.broadcasted_iota(jnp.int32, (half, 2 * RANK), 1) < RANK

    def packed(masked, height):
        both = nn_dot(masked, fold_matrix(height))
        return jnp.where(lane_low, both[:half], both[half:]).astype(BF16)

    def send_all(src, land, s, r, axis, index, count):
        copies = []
        for d in range(1, count):
            copy = remote(src, land.at[d - 1], s.at[d - 1], r.at[d - 1], axis, (index + d) % count)
            copy.start()
            copies.append(copy)
            sent.append(copy)
        return copies

    def total_of(src, land, copies):
        total = src[...].astype(F32)
        for d, copy in enumerate(copies):
            copy.wait_recv()
            total = total + land[d].astype(F32)
        return total

    def spread(short, width):
        both = jnp.concatenate(
            [nn_dot(short, spread_matrix(0)), nn_dot(short, spread_matrix(RANK))], axis=0
        )
        return jnp.concatenate([both] * (width // 2), axis=1)

    load_c.wait()
    part = nt_dot(call[...].reshape(R, C), up[...])
    pack[0] = packed((part * mup[...].astype(F32)).astype(BF16), nu * RANK)
    back_one = send_all(pack.at[0], brt, b1_s, b1_r, "tensor", t, T)
    if chunks > early:
        forward(chunks - 1)
    pack[2] = total_of(pack.at[0], brt, back_one).astype(BF16)
    back_two = send_all(pack.at[2], brj, b2_s, b2_r, "job", j, J)

    load_d.wait()
    for copy in forwards:
        copy.wait_recv()

    @pl.loop(0, J)
    def _(b):
        rows = pl.ds(pl.multiple_of(b * hr, hr), hr)
        value = nt_dot(hall[b], dnv[...])
        backcat[rows] = (value * mdn[rows].astype(F32)).astype(BF16)

    pack[1] = packed(backcat[...], nd * RANK)
    inner_one = send_all(pack.at[1], irj, i1_s, i1_r, "job", j, J)
    back = (adapter_scale * total_of(pack.at[2], brj, back_two)).astype(BF16)
    backcat[...] = (spread(back, nd) * mdn[...].astype(F32)).astype(BF16)

    blocks = 2 * hr // cr

    def mixed_copy(d, h):
        to = (t + d) % T
        cols = pl.ds(h * (C // 4), C // 4)
        return to, remote(
            mst.at[to, :, cols], mrv.at[d - 1, :, cols],
            ms.at[d - 1, h], mr.at[d - 1, h], "tensor", to,
        )

    def send_mixed(own, h):
        for d in range(1, T):
            to, copy = mixed_copy(d, h)

            @pl.when((to // blocks == px) if own else (to // blocks != px))
            def _():
                copy.start()

    def pair_rows(pair):
        return pl.ds(pl.multiple_of(pair * 2 * hr, 2 * hr), 2 * hr)

    def tile(k):
        return pl.ds(pl.multiple_of(k * ft, ft), ft)

    def pair_copy(k):
        return remote(
            bpb.at[:, 1 - c, :, tile(k)], prv.at[:, :, tile(k)], ps.at[k], pr.at[k], "job", partner
        )

    def outer_copy(d, k):
        to = (j + 2 * d) % J
        return remote(
            bpb.at[to // 2, c, :, tile(k)], xrv.at[d - 1, :, tile(k)],
            xs.at[d - 1, k], xr.at[d - 1, k], "job", to,
        )

    def pass_on(k):
        pair_copy(k).wait_recv()
        both = bpb[:, c, :, tile(k)].astype(F32) + prv[:, :, tile(k)].astype(F32)
        bpb[:, c, :, tile(k)] = both.astype(BF16)
        for d in range(1, NP):
            outer_copy(d, k).start()

    def backward(k):
        value = nt_dot(call[...].reshape(R, C), wv[tile(k)])
        value = value + nn_dot(backcat[...], dnv[:, tile(k)])
        bpb[:, :, :, tile(k)] = value.astype(BF16).reshape(NP, 2, hr, ft)
        pair_copy(k).start()
        grad = tn_dot(backcat[...], hall[:, :, tile(k)].reshape(R, ft))
        dnv[:, tile(k)] = grad.astype(BF16)

        @pl.when(k > 0)
        def _():
            pass_on(k - 1)

    def other_forward(n):
        for e in range(1, NP):
            pair = (px + e) % NP
            rows = hall[pl.ds(2 * pair, 2)].reshape(2 * hr, F)
            value = nn_dot(rows, wv[:, columns(n)])
            value = value + nn_dot(innercat[pair_rows(pair)], up[:, columns(n)])
            mst[pl.ds(pair * blocks, blocks), :, columns(n)] = value.astype(BF16).reshape(
                blocks, cr, ct
            )

    first = max(1, nft // 14)
    second = 2 * first
    pl.loop(0, first)(backward)
    pack[3] = total_of(pack.at[1], irj, inner_one).astype(BF16)
    inner_two = send_all(pack.at[3], irt, i2_s, i2_r, "tensor", t, T)
    pl.loop(first, second)(backward)
    inner = total_of(pack.at[3], irt, inner_two).astype(BF16)
    innercat[...] = (adapter_scale * spread(inner, nu) * mup[...].astype(F32)).astype(BF16)

    @pl.loop(0, nct)
    def _(n):
        value = fa[:, columns(n)] + nn_dot(innercat[pair_rows(px)], up[:, columns(n)])
        mst[pl.ds(px * blocks, blocks), :, columns(n)] = value.astype(BF16).reshape(blocks, cr, ct)

    for h in range(4):
        send_mixed(True, h)

    beside = nct <= nft - second

    def joint(n):
        other_forward(n)
        if beside:
            backward(second + n)

    for h in range(4):
        pl.loop(h * (nct // 4), (h + 1) * (nct // 4))(joint)
        send_mixed(False, h)
    third = second + nct if beside else second
    pl.loop(third, nft)(backward)
    pass_on(nft - 1)
    out_gd = pltpu.make_async_copy(dnv, gd, outs.at[0])
    out_gd.start()

    @pl.loop(0, nct)
    def _(n):
        cots = call[:, :, columns(n)].reshape(R, ct)
        ugv[:, columns(n)] = tn_dot(innercat[...], cots).astype(BF16)

    out_ug = pltpu.make_async_copy(ugv, ug, outs.at[1])
    out_ug.start()

    @pl.loop(0, nft)
    def _(k):
        value = bpb[px, c, :, tile(k)].astype(F32)
        for d in range(1, NP):
            outer_copy(d, k).wait_recv()
            value = value + xrv[d - 1, :, tile(k)].astype(F32)
        bpb[px, c, :, tile(k)] = value.astype(BF16)

    out_hg = pltpu.make_async_copy(bpb.at[px, c], hg, outs.at[2])
    out_hg.start()

    for h in range(4):
        for d in range(1, T):
            mixed_copy(d, h)[1].wait_recv()

        @pl.loop(h * (nct // 4), (h + 1) * (nct // 4))
        def _(n):
            value = mst[t, :, columns(n)].astype(F32)
            for d in range(1, T):
                value = value + mrv[d - 1, :, columns(n)].astype(F32)
            mst[t, :, columns(n)] = value.astype(BF16)

    out_mx = pltpu.make_async_copy(mst.at[t], mixed, outs.at[3])
    out_mx.start()

    for copy in sent:
        copy.wait_send()
    for step in range(T - 1):
        line_each(step, lambda copy: copy.wait_send(), False)
    for h in range(4):
        for d in range(1, T):
            mixed_copy(d, h)[1].wait_send()

    @pl.loop(0, nft)
    def _(k):
        pair_copy(k).wait_send()
        for d in range(1, NP):
            outer_copy(d, k).wait_send()

    out_gd.wait()
    out_ug.wait()
    out_hg.wait()
    out_mx.wait()


def per_device(hidden, weight, downs, ups, block_jobs, home, cotangent):
    hr, F = hidden.shape
    cr, C = cotangent.shape
    T = lax.axis_size("tensor")
    J = lax.axis_size("job")
    R = hr * J
    NP = J // 2
    nd, nu = downs.shape[0], ups.shape[0]
    ndl, nul = nd * RANK, nu * RANK
    dn = jnp.transpose(downs, (0, 2, 1)).reshape(ndl, F)
    up = ups.reshape(nul, C)
    ft = 512 if F % 512 == 0 else 128
    ct = 256
    chunks = 4 if F % 512 == 0 else 1
    nft = F // ft
    sem = pltpu.SemaphoreType.DMA
    anyspace = pl.BlockSpec(memory_space=pl.ANY)
    smem = pl.BlockSpec(memory_space=pltpu.SMEM)
    vmem = pl.BlockSpec(memory_space=pltpu.VMEM)
    n_out = max(NP - 1, 1)
    mixed, hg, gd, ug = pl.pallas_call(
        functools.partial(step_kernel, T, J, ft, ct, chunks),
        out_shape=(
            jax.ShapeDtypeStruct((cr, C), BF16),
            jax.ShapeDtypeStruct((hr, F), BF16),
            jax.ShapeDtypeStruct((ndl, F), BF16),
            jax.ShapeDtypeStruct((nul, C), BF16),
        ),
        in_specs=[anyspace, anyspace, anyspace, vmem, smem, smem, anyspace],
        out_specs=(anyspace,) * 4,
        scratch_shapes=[
            pltpu.VMEM((F, C), BF16),
            pltpu.VMEM((J, hr, F), BF16),
            pltpu.VMEM((T, cr, C), BF16),
            pltpu.VMEM((ndl, F), BF16),
            pltpu.VMEM((NP, 2, hr, F), BF16),
            pltpu.VMEM((NP, hr, F), BF16),
            pltpu.VMEM((n_out, hr, F), BF16),
            pltpu.VMEM((2 * hr, C), F32),
            pltpu.VMEM((T, cr, C), BF16),
            pltpu.VMEM((T - 1, cr, C), BF16),
            pltpu.VMEM((nul, C), BF16),
            pltpu.VMEM((R, ndl), BF16),
            pltpu.VMEM((R, nul), BF16),
            pltpu.VMEM((R, ndl), BF16),
            pltpu.VMEM((R, nul), BF16),
            pltpu.VMEM((4, R // 2, 2 * RANK), BF16),
            pltpu.VMEM((T - 1, R // 2, 2 * RANK), BF16),
            pltpu.VMEM((J - 1, R // 2, 2 * RANK), BF16),
            pltpu.VMEM((T - 1, R // 2, 2 * RANK), BF16),
            pltpu.VMEM((J - 1, R // 2, 2 * RANK), BF16),
            sem((4,)),
            sem((2, T - 1)), sem((2, T - 1)),
            sem((1,)), sem((1,)),
            sem((n_out, chunks)), sem((n_out, chunks)),
            sem((n_out, chunks)), sem((n_out, chunks)),
            sem((T - 1,)), sem((T - 1,)), sem((J - 1,)), sem((J - 1,)),
            sem((J - 1,)), sem((J - 1,)), sem((T - 1,)), sem((T - 1,)),
            sem((nft,)), sem((nft,)),
            sem((n_out, nft)), sem((n_out, nft)),
            sem((T - 1, 4)), sem((T - 1, 4)),
            sem((4,)),
        ],
        compiler_params=pltpu.CompilerParams(
            collective_id=0, has_side_effects=True, vmem_limit_bytes=64 * 1024 * 1024
        ),
    )(hidden, weight, dn, up, block_jobs, home, cotangent)
    grad_down = jnp.transpose(gd.reshape(nd, RANK, F), (0, 2, 1))
    return mixed, hg, grad_down, ug.reshape(nu, RANK, C)


def solution(mesh):
    in_specs = (
        P(("group", "job"), "tensor"),
        P("tensor", "job"),
        P(("group", "job"), "tensor", None),
        P(("group", "tensor"), None, "job"),
        P("group"),
        P("group"),
        P(("group", "tensor"), "job"),
    )
    out_specs = (
        P(("group", "tensor"), "job"),
        P(("group", "job"), "tensor"),
        P(("group", "job"), "tensor", None),
        P(("group", "tensor"), None, "job"),
    )
    return jax.shard_map(
        per_device, mesh=mesh, in_specs=in_specs, out_specs=out_specs, check_vma=False
    )
```
